32 devices in a mesh: tile: 8 (over y, x, core), subap: 4 (over z).
Axes of the slice: x: 2, y: 2, z: 4, core: 2. Of those that a mesh axis runs over, the one named last changes fastest.
Arguments:
- pulses: bfloat16 [8, 4, 2, 128, 16384], P('tile', 'subap'), may hold values from -6 to 6
- footprint: int32 [8, 4, 16], P('tile', 'subap'), may hold values from 0 to 23, as said below
- offsets: int32 [24], replicated, may hold values from 0 to 15872
- azimuth: bfloat16 [24, 8, 4, 2, 256, 128], P('tile', None, 'subap'), may hold values from -0.125 to 0.125
- range_interp: bfloat16 [24, 2, 512, 256], P('tile'), may hold values from -0.1875 to 0.1875
Outputs:
- image: float32 [24, 2, 256, 256], P('tile', None, 'subap')
The draws below stay inside these ranges and needn't reach their ends.
Inputs may be any that keep to these rules, and one draw needn't show every extreme that they name: For every o, footprint[k, s, o * 2 : (o + 1) * 2] holds 2 different tiles of o * 3 to (o + 1) * 3 - 1.
All inputs are finite; a program needn't handle non-finite values.
Results may differ from the reference program's by a relative error of at most 0.0029.
Values may be sent and summed in bfloat16 or wider, within the bound.
A program may use at most 128 MiB of HBM per device.

```python
import jax
import jax.numpy as jnp
from jax import lax

RANGE = 16384
PB = 128
RW = 512
TA = 256
TR = 256
TILE_DEV = 3
CAP = 2
TILES = 24
SRC = 8
SUBAPS = 4


def draw_footprint(key, part):
    owners = TILES // TILE_DEV
    popular = jax.random.randint(jax.random.fold_in(key, 7), (owners, TILE_DEV), 0, 4)
    noise = jax.random.randint(jax.random.fold_in(key, 11), (SRC, SUBAPS, owners, TILE_DEV), 0, 64)
    scores = (noise + 32 * popular[None, None]) * TILE_DEV + jnp.arange(TILE_DEV, dtype=jnp.int32)
    chosen = lax.top_k(scores, CAP)[1].astype(jnp.int32)
    tiles = chosen + (jnp.arange(owners, dtype=jnp.int32) * TILE_DEV)[None, None, :, None]
    return tiles.reshape(SRC, SUBAPS, owners * CAP).astype(jnp.int32)


def plant(values, stream_key, least, largest):
    extent = values.shape
    spot = [jax.random.randint(jax.random.fold_in(stream_key, axis), (), 0, extent[axis]) for axis in range(len(extent))]
    values = values.at[tuple(spot)].set(least)
    longest = extent.index(max(extent))
    spot[longest] = (spot[longest] + 1) % extent[longest]
    return values.at[tuple(spot)].set(largest)


def shard_levels(own_key, extent, cuts, low, largest):
    gain, own = 1.0, jax.random.fold_in(own_key, 6)
    for position, shards_of in cuts:
        steps = jnp.exp(jax.random.uniform(jax.random.fold_in(own, position), (shards_of,), jnp.float32, low / len(cuts), largest / len(cuts)))
        gain = gain * jnp.repeat(steps, extent[position] // shards_of).reshape([-1 if axis == position else 1 for axis in range(len(extent))])
    return gain


def bell_draw(own_key, dims, spread, most, cuts=(), kind=jnp.bfloat16):
    result = jax.random.normal(own_key, dims, jnp.float32) * spread
    if len(cuts) > 0:
        result = shard_levels(own_key, dims, cuts, -0.22, 0.18) * result
    return jnp.clip(result, min=-most, max=most).astype(kind)


def setup_inputs(seed: int = 0) -> dict:
    splits = jax.random.split(jax.random.key(seed), 6)
    return {
        "pulses": bell_draw(splits[0], (SRC, SUBAPS, 2, PB, RANGE), 1.0, 6.0, ((0, 8), (1, 4))),
        "footprint": draw_footprint(jax.random.fold_in(splits[5], 71), 0),
        "offsets": plant(jax.random.randint(splits[2], (TILES,), 0, RANGE - RW + 1), jax.random.fold_in(splits[2], 1), 0, RANGE - RW).astype(jnp.int32),
        "azimuth": bell_draw(splits[3], (TILES, SRC, SUBAPS, 2, TA, PB), (2 * SRC * PB) ** -0.5, 0.125, ((0, 8), (2, 4))),
        "range_interp": bell_draw(splits[4], (TILES, 2, RW, TR), (2 * RW) ** -0.5, 0.1875, ((0, 8),)),
    }


def combine(prod):
    real = prod[..., 0, 0, :, :] - prod[..., 1, 1, :, :]
    imag = prod[..., 0, 1, :, :] + prod[..., 1, 0, :, :]
    return jnp.stack([real, imag], axis=-3)

def reference(pulses, footprint, offsets, azimuth, range_interp):

    def one_tile(items):
        index, start, tile_az, table = items
        zero = jnp.zeros((), jnp.int32)
        window = lax.dynamic_slice(pulses, (zero, zero, zero, zero, start.astype(jnp.int32)), (SRC, SUBAPS, 2, PB, RW))
        hit = jnp.any(footprint == index, axis=-1).astype(pulses.dtype)
        window = window * hit[:, :, None, None, None]
        prod = jnp.einsum('kscpr,dru->kscdpu', window.astype(jnp.float32), table.astype(jnp.float32))
        ranged = combine(prod).astype(jnp.bfloat16)
        sub = combine(jnp.einsum('kscap,ksdpu->scdau', tile_az.astype(jnp.float32), ranged.astype(jnp.float32)))
        raw = lax.optimization_barrier(jnp.sum(sub, axis=0))
        power = jnp.mean(raw * raw)
        return raw / jnp.sqrt(power + 1e-06)
    tile_ids = jnp.arange(TILES, dtype=jnp.int32)
    return lax.map(one_tile, (tile_ids, offsets, azimuth, range_interp))
```

```python
import functools

import jax
import jax.numpy as jnp
from jax import lax
from jax.experimental import pallas as pl
from jax.experimental.pallas import tpu as pltpu
from jax.sharding import PartitionSpec as P

MESH = pl.DeviceIdType.MESH
LANES = 128
FLAG_ROWS = 16
CHUNK = 32


def stage_at(slot, rows):
    start = slot * rows + (FLAG_ROWS if slot > 0 else 0)
    size = rows + (FLAG_ROWS if slot == 0 else 0)
    return start, size


def cut_kernel(dims, feet, offs, pulses, out, block, load_sem):
    n, ns, tdev, cap = dims
    rows, reach = block.shape
    width = out.shape[2]
    slab = width + LANES
    d = pl.program_id(0)
    me = lax.axis_index("tile")
    load = pltpu.make_async_copy(pulses, block, load_sem)

    @pl.when(d == 0)
    def _():
        load.start()
        load.wait()

    lane = lax.broadcasted_iota(jnp.int32, (CHUNK, LANES), 1)
    flag_row = lax.broadcasted_iota(jnp.int32, (FLAG_ROWS, width), 0)
    owner = lax.rem(me + d, n)
    first, second = feet[owner * cap], feet[owner * cap + 1]
    low, high = jnp.minimum(first, second), jnp.maximum(first, second)
    for slot in range(cap):
        start = offs[high if slot else low]
        base = jnp.minimum((start // LANES) * LANES, reach - slab)
        base = pl.multiple_of(base, LANES)
        shift = start - base
        turn = lax.rem(LANES - shift + LANES, LANES)
        keep = lane < LANES - shift
        place = stage_at(slot, rows)[0]
        for r in range(0, rows, CHUNK):
            x = block[pl.ds(r, CHUNK), pl.ds(base, slab)].astype(jnp.float32)
            turned = [
                pltpu.roll(x[:, c * LANES:(c + 1) * LANES], turn, 1) for c in range(slab // LANES)
            ]
            y = [jnp.where(keep, turned[c], turned[c + 1]) for c in range(width // LANES)]
            out[0, pl.ds(place + r, CHUNK)] = jnp.concatenate(y, axis=1).astype(jnp.bfloat16)
    mine = owner * tdev
    hit = (flag_row == low - mine) | (flag_row == tdev + high - mine)
    out[0, pl.ds(rows, FLAG_ROWS)] = jnp.where(hit, 1.0, 0.0).astype(jnp.bfloat16)


def kernel(dims, send, azimuth, interp, out, az, table, recv, acc,
           zsend, zrecv, psend, precv, load_sem, send_sem, recv_sem, zsend_sem, zrecv_sem, psend_sem, precv_sem):
    n, ns, tdev, cap = dims
    half = az.shape[4]
    rows = 2 * half
    ta, two_tr = acc.shape[1:]
    tr = two_tr // 2
    height = ta // ns
    me = lax.axis_index("tile")
    mz = lax.axis_index("subap")

    loads = [
        pltpu.make_async_copy(src, dst, load_sem.at[i])
        for i, (src, dst) in enumerate(((send.at[0], recv.at[0]), (interp, table), (azimuth, az)))
    ]
    for load in loads:
        load.start()

    barrier = pltpu.get_barrier_semaphore()
    for d in range(1, n):
        pl.semaphore_signal(barrier, inc=1, device_id={"tile": lax.rem(me + d, n)}, device_id_type=MESH)
    for e in range(1, ns):
        pl.semaphore_signal(barrier, inc=1, device_id={"subap": lax.rem(mz + e, ns)}, device_id_type=MESH)

    def window_copy(d, slot):
        start, size = stage_at(slot, rows)
        return pltpu.make_async_remote_copy(
            src_ref=send.at[d, pl.ds(start, size)],
            dst_ref=recv.at[d, pl.ds(start, size)],
            send_sem=send_sem.at[d, slot],
            recv_sem=recv_sem.at[d, slot],
            device_id={"tile": lax.rem(me + d, n)},
            device_id_type=MESH,
        )

    pl.semaphore_wait(barrier, n + ns - 2)
    for slot in range(cap):
        def issue(i, carry, slot=slot):
            window_copy(n - i, slot).start()
            return carry
        lax.fori_loop(1, n, issue, 0)
    for load in loads:
        load.wait()

    def add(buf, d, t):
        flags = buf[d, pl.ds(rows, FLAG_ROWS)].astype(jnp.float32)
        w = None
        for slot in range(cap):
            if slot <= t <= tdev - cap + slot:
                row = slot * tdev + t
                term = buf[d, pl.ds(stage_at(slot, rows)[0], rows)] * flags[row:row + 1].astype(jnp.bfloat16)
                w = term if w is None else w + term
        pr = jnp.dot(w, table[t, 0], preferred_element_type=jnp.float32)
        pi = jnp.dot(w, table[t, 1], preferred_element_type=jnp.float32)
        rr = (pr[:half] - pi[half:]).astype(jnp.bfloat16)
        ri = (pi[:half] + pr[half:]).astype(jnp.bfloat16)
        right = jnp.concatenate(
            [jnp.concatenate([rr, ri], axis=1), jnp.concatenate([-ri, rr], axis=1)], axis=0
        )
        k = lax.rem(me - d + n, n)
        left = jnp.concatenate([az[t, k, 0], az[t, k, 1]], axis=1)
        return jnp.dot(left, right, preferred_element_type=jnp.float32)

    def image_copy(e, t):
        dest = lax.rem(mz + e, ns)
        return pltpu.make_async_remote_copy(
            src_ref=zsend.at[t, pl.ds(pl.multiple_of(dest * height, height), height)],
            dst_ref=zrecv.at[e, t],
            send_sem=zsend_sem.at[e, t],
            recv_sem=zrecv_sem.at[e, t],
            device_id={"subap": dest},
            device_id_type=MESH,
        )

    for t in range(tdev):
        acc[t] = add(recv, 0, t)
    for slot in range(cap):
        done = [t for t in range(tdev) if min(t, cap - 1) == slot]

        def gather(d, carry, slot=slot, done=done):
            window_copy(d, slot).wait_recv()
            for t in done:
                acc[t] += add(recv, d, t)
            return carry
        lax.fori_loop(1, n, gather, 0)
        for t in done:
            zsend[t] = acc[t].astype(jnp.bfloat16)
            for e in range(1, ns):
                image_copy(e, t).start()

    own = pl.ds(pl.multiple_of(mz * height, height), height)
    raw = []
    for t in range(tdev):
        x = acc[t, own]
        for e in range(1, ns):
            image_copy(e, t).wait_recv()
            x = x + zrecv[e, t].astype(jnp.float32)
        zraw = jnp.sum(x * x, axis=0, keepdims=True)
        fold = sum(zraw[:, c:c + LANES] for c in range(0, two_tr, LANES))
        psend[t] = jnp.broadcast_to(fold, (8, LANES))
        acc[t, own] = x

    def power_copy(e):
        return pltpu.make_async_remote_copy(
            src_ref=psend,
            dst_ref=precv.at[e],
            send_sem=psend_sem.at[e],
            recv_sem=precv_sem.at[e],
            device_id={"subap": lax.rem(mz + e, ns)},
            device_id_type=MESH,
        )

    for e in range(1, ns):
        power_copy(e).start()
    for e in range(1, ns):
        power_copy(e).wait_recv()
    for t in range(tdev):
        total = psend[t]
        for e in range(1, ns):
            total = total + precv[e, t]
        power = jnp.sum(total[:1], axis=1, keepdims=True) / (ta * two_tr)
        x = acc[t, own] / jnp.sqrt(power + 1e-06)
        out[t, 0] = x[:, :tr]
        out[t, 1] = x[:, tr:]

    for slot in range(cap):
        def drain(d, carry, slot=slot):
            window_copy(d, slot).wait_send()
            return carry
        lax.fori_loop(1, n, drain, 0)
    for e in range(1, ns):
        power_copy(e).wait_send()
        for t in range(tdev):
            image_copy(e, t).wait_send()


def on_device(pulses, footprint, offsets, azimuth, range_interp):
    n, ns = lax.axis_size("tile"), lax.axis_size("subap")
    tdev = azimuth.shape[0]
    cap = footprint.shape[2] // n
    rows = 2 * pulses.shape[3]
    width, tr = range_interp.shape[2:]
    ta = azimuth.shape[4]
    height = ta // ns
    stage = cap * rows + FLAG_ROWS
    dma = pltpu.SemaphoreType.DMA
    smem = pl.BlockSpec(memory_space=pltpu.SMEM)
    hbm = pl.BlockSpec(memory_space=pl.ANY)
    dims = (n, ns, tdev, cap)
    send = pl.pallas_call(
        functools.partial(cut_kernel, dims),
        grid=(n,),
        out_shape=jax.ShapeDtypeStruct((n, stage, width), jnp.bfloat16),
        in_specs=[smem, smem, hbm],
        out_specs=pl.BlockSpec((1, stage, width), lambda d: (d, 0, 0)),
        scratch_shapes=[pltpu.VMEM((rows, pulses.shape[4]), jnp.bfloat16), dma],
        compiler_params=pltpu.CompilerParams(vmem_limit_bytes=52 * 1024 * 1024),
        cost_estimate=pl.CostEstimate(flops=10_000_000, bytes_accessed=13_000_000, transcendentals=0),
    )(footprint.reshape(-1), offsets, pulses.reshape(rows, pulses.shape[4]))
    return pl.pallas_call(
        functools.partial(kernel, dims),
        out_shape=jax.ShapeDtypeStruct((tdev, 2, height, tr), jnp.float32),
        in_specs=[hbm, hbm, hbm],
        out_specs=pl.BlockSpec(memory_space=pltpu.VMEM),
        scratch_shapes=[
            pltpu.VMEM((tdev, n, 2, ta, rows // 2), jnp.bfloat16),
            pltpu.VMEM((tdev, 2, width, tr), jnp.bfloat16),
            pltpu.VMEM((n, stage, width), jnp.bfloat16),
            pltpu.VMEM((tdev, ta, 2 * tr), jnp.float32),
            pltpu.VMEM((tdev, ta, 2 * tr), jnp.bfloat16),
            pltpu.VMEM((ns, tdev, height, 2 * tr), jnp.bfloat16),
            pltpu.VMEM((tdev, 8, LANES), jnp.float32),
            pltpu.VMEM((ns, tdev, 8, LANES), jnp.float32),
            dma((3,)),
            dma((n, cap)),
            dma((n, cap)),
            dma((ns, tdev)),
            dma((ns, tdev)),
            dma((ns,)),
            dma((ns,)),
        ],
        compiler_params=pltpu.CompilerParams(
            collective_id=0, has_side_effects=True, vmem_limit_bytes=52 * 1024 * 1024
        ),
        cost_estimate=pl.CostEstimate(flops=5_000_000_000, bytes_accessed=14_000_000, transcendentals=0),
    )(send, azimuth[:, :, 0], range_interp)


def solution(mesh):
    in_specs = (
        P("tile", "subap", None, None, None),
        P("tile", "subap", None),
        P(),
        P("tile", None, "subap", None, None, None),
        P("tile", None, None, None),
    )
    out_specs = P("tile", None, "subap", None)
    return jax.shard_map(
        on_device, mesh=mesh, in_specs=in_specs, out_specs=out_specs, check_vma=False
    )
```

```python
import functools

import jax
import jax.numpy as jnp
from jax import lax
from jax.experimental import pallas as pl
from jax.experimental.pallas import tpu as pltpu
from jax.sharding import PartitionSpec as P

MESH = pl.DeviceIdType.MESH
LANES = 128
FLAG_ROWS = 16


def kernel(dims, info, pulses, azimuth, interp, out, block, az, table, send, recv, acc,
           zsend, zrecv, psend, precv, load_sem, column_sem, send_sem, recv_sem, zsend_sem, zrecv_sem, psend_sem, precv_sem):
    n, ns, tdev, cap = dims
    columns, rows = block.shape[:2]
    half = rows // 2
    width = recv.shape[2]
    ta, two_tr = acc.shape[1:]
    tr = two_tr // 2
    height = ta // ns
    me = lax.axis_index("tile")
    mz = lax.axis_index("subap")

    loads = [
        pltpu.make_async_copy(src, dst, load_sem.at[i])
        for i, (src, dst) in enumerate(((interp, table), (azimuth, az)))
    ]

    def column_copy(c):
        return pltpu.make_async_copy(
            pulses.at[:, pl.ds(pl.multiple_of(c * LANES, LANES), LANES)], block.at[c], column_sem.at[c]
        )

    def fetch(c, carry):
        column_copy(c).start()
        return carry

    def fetched(c, carry):
        column_copy(c).wait()
        return carry

    lax.fori_loop(0, columns, fetch, 0)
    for load in loads:
        load.start()

    barrier = pltpu.get_barrier_semaphore()
    for d in range(1, n):
        pl.semaphore_signal(barrier, inc=1, device_id={"tile": lax.rem(me + d, n)}, device_id_type=MESH)
    for e in range(1, ns):
        pl.semaphore_signal(barrier, inc=1, device_id={"subap": lax.rem(mz + e, ns)}, device_id_type=MESH)

    def at(slot):
        start = slot * rows + (FLAG_ROWS if slot > 0 else 0)
        size = rows + (FLAG_ROWS if slot == 0 else 0)
        return start, size

    def window_copy(d, slot):
        start, size = at(slot)
        return pltpu.make_async_remote_copy(
            src_ref=send.at[d, pl.ds(start, size)],
            dst_ref=recv.at[d, pl.ds(start, size)],
            send_sem=send_sem.at[d, slot],
            recv_sem=recv_sem.at[d, slot],
            device_id={"tile": lax.rem(me + d, n)},
            device_id_type=MESH,
        )

    taken = lax.broadcasted_iota(jnp.int32, (2 * LANES, LANES), 0) - lax.broadcasted_iota(
        jnp.int32, (2 * LANES, LANES), 1
    )
    flag_row = lax.broadcasted_iota(jnp.int32, (FLAG_ROWS, width), 0)

    def cut(d, slot):
        owner = lax.rem(me + d, n)
        entry = owner * cap + slot
        base, shift = info[entry], info[n * cap + entry]
        pick = jnp.where(taken == shift, 1.0, 0.0).astype(jnp.bfloat16)
        place = at(slot)[0]
        x = [block[base + c] for c in range(width // LANES + 1)]
        for c in range(width // LANES):
            pair = jnp.concatenate(x[c:c + 2], axis=1)
            y = jnp.dot(pair, pick, preferred_element_type=jnp.float32)
            send[d, pl.ds(place, rows), c * LANES:(c + 1) * LANES] = y.astype(jnp.bfloat16)
        if slot == 0:
            low, high = info[2 * n * cap + entry], info[2 * n * cap + entry + 1]
            hit = (flag_row == low) | (flag_row == tdev + high)
            send[d, pl.ds(rows, FLAG_ROWS)] = jnp.where(hit, 1.0, 0.0).astype(jnp.bfloat16)

    lax.fori_loop(0, columns, fetched, 0)
    pl.semaphore_wait(barrier, n + ns - 2)
    for slot in range(cap):
        def issue(i, carry, slot=slot):
            cut(n - i, slot)
            window_copy(n - i, slot).start()
            return carry
        lax.fori_loop(1, n, issue, 0)
    for slot in range(cap):
        cut(0, slot)
    for load in loads:
        load.wait()

    def add(buf, d, t):
        flags = buf[d, pl.ds(rows, FLAG_ROWS)].astype(jnp.float32)
        w = None
        for slot in range(cap):
            if slot <= t <= tdev - cap + slot:
                row = slot * tdev + t
                term = buf[d, pl.ds(at(slot)[0], rows)] * flags[row:row + 1].astype(jnp.bfloat16)
                w = term if w is None else w + term
        pr = jnp.dot(w, table[t, 0], preferred_element_type=jnp.float32)
        pi = jnp.dot(w, table[t, 1], preferred_element_type=jnp.float32)
        rr = (pr[:half] - pi[half:]).astype(jnp.bfloat16)
        ri = (pi[:half] + pr[half:]).astype(jnp.bfloat16)
        right = jnp.concatenate(
            [jnp.concatenate([rr, ri], axis=1), jnp.concatenate([-ri, rr], axis=1)], axis=0
        )
        k = lax.rem(me - d + n, n)
        left = jnp.concatenate([az[t, k, 0], az[t, k, 1]], axis=1)
        return jnp.dot(left, right, preferred_element_type=jnp.float32)

    def image_copy(e, t):
        dest = lax.rem(mz + e, ns)
        return pltpu.make_async_remote_copy(
            src_ref=zsend.at[t, pl.ds(pl.multiple_of(dest * height, height), height)],
            dst_ref=zrecv.at[e, t],
            send_sem=zsend_sem.at[e, t],
            recv_sem=zrecv_sem.at[e, t],
            device_id={"subap": dest},
            device_id_type=MESH,
        )

    for t in range(tdev):
        acc[t] = add(send, 0, t)
    for slot in range(cap):
        done = [t for t in range(tdev) if min(t, cap - 1) == slot]

        def gather(d, carry, slot=slot, done=done):
            window_copy(d, slot).wait_recv()
            for t in done:
                acc[t] += add(recv, d, t)
            return carry
        lax.fori_loop(1, n, gather, 0)
        for t in done:
            zsend[t] = acc[t].astype(jnp.bfloat16)
            for e in range(1, ns):
                image_copy(e, t).start()

    own = pl.ds(pl.multiple_of(mz * height, height), height)
    raw = []
    for t in range(tdev):
        x = acc[t, own]
        for e in range(1, ns):
            image_copy(e, t).wait_recv()
            x = x + zrecv[e, t].astype(jnp.float32)
        zraw = jnp.sum(x * x, axis=0, keepdims=True)
        fold = sum(zraw[:, c:c + LANES] for c in range(0, two_tr, LANES))
        psend[t] = jnp.broadcast_to(fold, (8, LANES))
        acc[t, own] = x

    def power_copy(e):
        return pltpu.make_async_remote_copy(
            src_ref=psend,
            dst_ref=precv.at[e],
            send_sem=psend_sem.at[e],
            recv_sem=precv_sem.at[e],
            device_id={"subap": lax.rem(mz + e, ns)},
            device_id_type=MESH,
        )

    for e in range(1, ns):
        power_copy(e).start()
    for e in range(1, ns):
        power_copy(e).wait_recv()
    for t in range(tdev):
        total = psend[t]
        for e in range(1, ns):
            total = total + precv[e, t]
        power = jnp.sum(total[:1], axis=1, keepdims=True) / (ta * two_tr)
        x = acc[t, own] / jnp.sqrt(power + 1e-06)
        out[t, 0] = x[:, :tr]
        out[t, 1] = x[:, tr:]

    for slot in range(cap):
        def drain(d, carry, slot=slot):
            window_copy(d, slot).wait_send()
            return carry
        lax.fori_loop(1, n, drain, 0)
    for e in range(1, ns):
        power_copy(e).wait_send()
        for t in range(tdev):
            image_copy(e, t).wait_send()


def on_device(pulses, footprint, offsets, azimuth, range_interp):
    n, ns = lax.axis_size("tile"), lax.axis_size("subap")
    tdev = azimuth.shape[0]
    cap = footprint.shape[2] // n
    rows = 2 * pulses.shape[3]
    width, tr = range_interp.shape[2:]
    ta = azimuth.shape[4]
    height = ta // ns
    stage = cap * rows + FLAG_ROWS
    columns = pulses.shape[4] // LANES
    feet = footprint.reshape(n, cap)
    low, high = jnp.min(feet, axis=1), jnp.max(feet, axis=1)
    tiles = jnp.stack([low, high], axis=1).reshape(-1)
    ids = jnp.arange(offsets.shape[0], dtype=jnp.int32)
    start = jnp.sum(jnp.where(tiles[:, None] == ids[None], offsets[None], 0), axis=1)
    base = jnp.minimum(start // LANES, columns - width // LANES - 1)
    local = tiles - jnp.repeat(jnp.arange(n, dtype=jnp.int32), cap) * tdev
    info = jnp.concatenate([base, start - base * LANES, local])
    dma = pltpu.SemaphoreType.DMA
    smem = pl.BlockSpec(memory_space=pltpu.SMEM)
    hbm = pl.BlockSpec(memory_space=pl.ANY)
    return pl.pallas_call(
        functools.partial(kernel, (n, ns, tdev, cap)),
        out_shape=jax.ShapeDtypeStruct((tdev, 2, height, tr), jnp.float32),
        in_specs=[smem, hbm, hbm, hbm],
        out_specs=pl.BlockSpec(memory_space=pltpu.VMEM),
        scratch_shapes=[
            pltpu.VMEM((columns, rows, LANES), jnp.bfloat16),
            pltpu.VMEM((tdev, n, 2, ta, rows // 2), jnp.bfloat16),
            pltpu.VMEM((tdev, 2, width, tr), jnp.bfloat16),
            pltpu.VMEM((n, stage, width), jnp.bfloat16),
            pltpu.VMEM((n, stage, width), jnp.bfloat16),
            pltpu.VMEM((tdev, ta, 2 * tr), jnp.float32),
            pltpu.VMEM((tdev, ta, 2 * tr), jnp.bfloat16),
            pltpu.VMEM((ns, tdev, height, 2 * tr), jnp.bfloat16),
            pltpu.VMEM((tdev, 8, LANES), jnp.float32),
            pltpu.VMEM((ns, tdev, 8, LANES), jnp.float32),
            dma((2,)),
            dma((columns,)),
            dma((n, cap)),
            dma((n, cap)),
            dma((ns, tdev)),
            dma((ns, tdev)),
            dma((ns,)),
            dma((ns,)),
        ],
        compiler_params=pltpu.CompilerParams(
            collective_id=0, has_side_effects=True, vmem_limit_bytes=52 * 1024 * 1024
        ),
        cost_estimate=pl.CostEstimate(flops=5_000_000_000, bytes_accessed=14_000_000, transcendentals=0),
    )(info, pulses.reshape(rows, pulses.shape[4]), azimuth[:, :, 0], range_interp)


def solution(mesh):
    in_specs = (
        P("tile", "subap", None, None, None),
        P("tile", "subap", None),
        P(),
        P("tile", None, "subap", None, None, None),
        P("tile", None, None, None),
    )
    out_specs = P("tile", None, "subap", None)
    return jax.shard_map(
        on_device, mesh=mesh, in_specs=in_specs, out_specs=out_specs, check_vma=False
    )
```

```python
import functools

import jax
import jax.numpy as jnp
from jax import lax
from jax.experimental import pallas as pl
from jax.experimental.pallas import tpu as pltpu
from jax.sharding import PartitionSpec as P

MESH = pl.DeviceIdType.MESH
LANES = 128
FLAG_ROWS = 16


def plan_kernel(dims, last, feet, offs, info):
    n, tdev, cap = dims
    for owner in range(n):
        first, second = feet[owner * cap], feet[owner * cap + 1]
        for slot in range(cap):
            entry = owner * cap + slot
            tile = jnp.maximum(first, second) if slot else jnp.minimum(first, second)
            start = offs[tile]
            base = jnp.minimum(lax.div(start, LANES), last)
            info[entry] = base
            info[n * cap + entry] = start - base * LANES
            info[2 * n * cap + entry] = tile - owner * tdev


def kernel(dims, info, pulses, azimuth, interp, out, block, az, table, send, recv, acc,
           zsend, zrecv, psend, precv, load_sem, column_sem, send_sem, recv_sem, zsend_sem, zrecv_sem, psend_sem, precv_sem):
    n, ns, tdev, cap = dims
    columns, rows = block.shape[:2]
    half = rows // 2
    width = recv.shape[2]
    ta, two_tr = acc.shape[1:]
    tr = two_tr // 2
    height = ta // ns
    me = lax.axis_index("tile")
    mz = lax.axis_index("subap")

    loads = [
        pltpu.make_async_copy(src, dst, load_sem.at[i])
        for i, (src, dst) in enumerate(((interp, table), (azimuth, az)))
    ]

    def column_copy(c):
        return pltpu.make_async_copy(
            pulses.at[:, pl.ds(pl.multiple_of(c * LANES, LANES), LANES)], block.at[c], column_sem.at[c]
        )

    def fetch(c, carry):
        column_copy(c).start()
        return carry

    def fetched(c, carry):
        column_copy(c).wait()
        return carry

    lax.fori_loop(0, columns, fetch, 0)
    for load in loads:
        load.start()

    barrier = pltpu.get_barrier_semaphore()
    for d in range(1, n):
        pl.semaphore_signal(barrier, inc=1, device_id={"tile": lax.rem(me + d, n)}, device_id_type=MESH)
    for e in range(1, ns):
        pl.semaphore_signal(barrier, inc=1, device_id={"subap": lax.rem(mz + e, ns)}, device_id_type=MESH)

    def at(slot):
        start = slot * rows + (FLAG_ROWS if slot > 0 else 0)
        size = rows + (FLAG_ROWS if slot == 0 else 0)
        return start, size

    def window_copy(d, slot):
        start, size = at(slot)
        return pltpu.make_async_remote_copy(
            src_ref=send.at[d, pl.ds(start, size)],
            dst_ref=recv.at[d, pl.ds(start, size)],
            send_sem=send_sem.at[d, slot],
            recv_sem=recv_sem.at[d, slot],
            device_id={"tile": lax.rem(me + d, n)},
            device_id_type=MESH,
        )

    taken = lax.broadcasted_iota(jnp.int32, (2 * LANES, LANES), 0) - lax.broadcasted_iota(
        jnp.int32, (2 * LANES, LANES), 1
    )
    flag_row = lax.broadcasted_iota(jnp.int32, (FLAG_ROWS, width), 0)

    def cut(d, slot):
        owner = lax.rem(me + d, n)
        entry = owner * cap + slot
        base, shift = info[entry], info[n * cap + entry]
        pick = jnp.where(taken == shift, 1.0, 0.0).astype(jnp.bfloat16)
        place = at(slot)[0]
        x = [block[base + c] for c in range(width // LANES + 1)]
        for c in range(width // LANES):
            pair = jnp.concatenate(x[c:c + 2], axis=1)
            y = jnp.dot(pair, pick, preferred_element_type=jnp.float32)
            send[d, pl.ds(place, rows), c * LANES:(c + 1) * LANES] = y.astype(jnp.bfloat16)
        if slot == 0:
            low, high = info[2 * n * cap + entry], info[2 * n * cap + entry + 1]
            hit = (flag_row == low) | (flag_row == tdev + high)
            send[d, pl.ds(rows, FLAG_ROWS)] = jnp.where(hit, 1.0, 0.0).astype(jnp.bfloat16)

    lax.fori_loop(0, columns, fetched, 0)
    pl.semaphore_wait(barrier, n + ns - 2)
    for slot in range(cap):
        def issue(i, carry, slot=slot):
            cut(n - i, slot)
            if slot == 0:
                window_copy(n - i, slot).start()
            return carry
        lax.fori_loop(1, n, issue, 0)
    for slot in range(cap):
        cut(0, slot)
    for load in loads:
        load.wait()

    def add(buf, d, t):
        flags = buf[d, pl.ds(rows, FLAG_ROWS)].astype(jnp.float32)
        w = None
        for slot in range(cap):
            if slot <= t <= tdev - cap + slot:
                row = slot * tdev + t
                term = buf[d, pl.ds(at(slot)[0], rows)] * flags[row:row + 1].astype(jnp.bfloat16)
                w = term if w is None else w + term
        pr = jnp.dot(w, table[t, 0], preferred_element_type=jnp.float32)
        pi = jnp.dot(w, table[t, 1], preferred_element_type=jnp.float32)
        rr = (pr[:half] - pi[half:]).astype(jnp.bfloat16)
        ri = (pi[:half] + pr[half:]).astype(jnp.bfloat16)
        right = jnp.concatenate(
            [jnp.concatenate([rr, ri], axis=1), jnp.concatenate([-ri, rr], axis=1)], axis=0
        )
        k = lax.rem(me - d + n, n)
        left = jnp.concatenate([az[t, k, 0], az[t, k, 1]], axis=1)
        return jnp.dot(left, right, preferred_element_type=jnp.float32)

    def image_copy(e, t):
        dest = lax.rem(mz + e, ns)
        return pltpu.make_async_remote_copy(
            src_ref=zsend.at[t, pl.ds(pl.multiple_of(dest * height, height), height)],
            dst_ref=zrecv.at[e, t],
            send_sem=zsend_sem.at[e, t],
            recv_sem=zrecv_sem.at[e, t],
            device_id={"subap": dest},
            device_id_type=MESH,
        )

    for t in range(tdev):
        acc[t] = add(send, 0, t)
    for slot in range(cap):
        if slot + 1 < cap:
            def follow(i, carry, slot=slot):
                window_copy(n - i, slot).wait_send()
                window_copy(n - i, slot + 1).start()
                return carry
            lax.fori_loop(1, n, follow, 0)
        done = [t for t in range(tdev) if min(t, cap - 1) == slot]

        def gather(d, carry, slot=slot, done=done):
            window_copy(d, slot).wait_recv()
            for t in done:
                acc[t] += add(recv, d, t)
            return carry
        lax.fori_loop(1, n, gather, 0)
        for t in done:
            zsend[t] = acc[t].astype(jnp.bfloat16)
            for e in range(1, ns):
                image_copy(e, t).start()

    own = pl.ds(pl.multiple_of(mz * height, height), height)
    raw = []
    for t in range(tdev):
        x = acc[t, own]
        for e in range(1, ns):
            image_copy(e, t).wait_recv()
            x = x + zrecv[e, t].astype(jnp.float32)
        zraw = jnp.sum(x * x, axis=0, keepdims=True)
        fold = sum(zraw[:, c:c + LANES] for c in range(0, two_tr, LANES))
        psend[t] = jnp.broadcast_to(fold, (8, LANES))
        acc[t, own] = x

    def power_copy(e):
        return pltpu.make_async_remote_copy(
            src_ref=psend,
            dst_ref=precv.at[e],
            send_sem=psend_sem.at[e],
            recv_sem=precv_sem.at[e],
            device_id={"subap": lax.rem(mz + e, ns)},
            device_id_type=MESH,
        )

    for e in range(1, ns):
        power_copy(e).start()
    for e in range(1, ns):
        power_copy(e).wait_recv()
    for t in range(tdev):
        total = psend[t]
        for e in range(1, ns):
            total = total + precv[e, t]
        power = jnp.sum(total[:1], axis=1, keepdims=True) / (ta * two_tr)
        x = acc[t, own] / jnp.sqrt(power + 1e-06)
        out[t, 0] = x[:, :tr]
        out[t, 1] = x[:, tr:]

    def drain(d, carry):
        window_copy(d, cap - 1).wait_send()
        return carry
    lax.fori_loop(1, n, drain, 0)
    for e in range(1, ns):
        power_copy(e).wait_send()
        for t in range(tdev):
            image_copy(e, t).wait_send()


def on_device(pulses, footprint, offsets, azimuth, range_interp):
    n, ns = lax.axis_size("tile"), lax.axis_size("subap")
    tdev = azimuth.shape[0]
    cap = footprint.shape[2] // n
    rows = 2 * pulses.shape[3]
    width, tr = range_interp.shape[2:]
    ta = azimuth.shape[4]
    height = ta // ns
    stage = cap * rows + FLAG_ROWS
    columns = pulses.shape[4] // LANES
    dma = pltpu.SemaphoreType.DMA
    smem = pl.BlockSpec(memory_space=pltpu.SMEM)
    hbm = pl.BlockSpec(memory_space=pl.ANY)
    info = pl.pallas_call(
        functools.partial(plan_kernel, (n, tdev, cap), columns - width // LANES - 1),
        out_shape=jax.ShapeDtypeStruct((3 * n * cap,), jnp.int32),
        in_specs=[smem, smem],
        out_specs=smem,
    )(footprint.reshape(-1), offsets)
    return pl.pallas_call(
        functools.partial(kernel, (n, ns, tdev, cap)),
        out_shape=jax.ShapeDtypeStruct((tdev, 2, height, tr), jnp.float32),
        in_specs=[smem, hbm, hbm, hbm],
        out_specs=pl.BlockSpec(memory_space=pltpu.VMEM),
        scratch_shapes=[
            pltpu.VMEM((columns, rows, LANES), jnp.bfloat16),
            pltpu.VMEM((tdev, n, 2, ta, rows // 2), jnp.bfloat16),
            pltpu.VMEM((tdev, 2, width, tr), jnp.bfloat16),
            pltpu.VMEM((n, stage, width), jnp.bfloat16),
            pltpu.VMEM((n, stage, width), jnp.bfloat16),
            pltpu.VMEM((tdev, ta, 2 * tr), jnp.float32),
            pltpu.VMEM((tdev, ta, 2 * tr), jnp.bfloat16),
            pltpu.VMEM((ns, tdev, height, 2 * tr), jnp.bfloat16),
            pltpu.VMEM((tdev, 8, LANES), jnp.float32),
            pltpu.VMEM((ns, tdev, 8, LANES), jnp.float32),
            dma((2,)),
            dma((columns,)),
            dma((n, cap)),
            dma((n, cap)),
            dma((ns, tdev)),
            dma((ns, tdev)),
            dma((ns,)),
            dma((ns,)),
        ],
        compiler_params=pltpu.CompilerParams(
            collective_id=0, has_side_effects=True, vmem_limit_bytes=62 * 1024 * 1024
        ),
        cost_estimate=pl.CostEstimate(flops=5_000_000_000, bytes_accessed=14_000_000, transcendentals=0),
    )(info, pulses.reshape(rows, pulses.shape[4]), azimuth[:, :, 0], range_interp)


def solution(mesh):
    in_specs = (
        P("tile", "subap", None, None, None),
        P("tile", "subap", None),
        P(),
        P("tile", None, "subap", None, None, None),
        P("tile", None, None, None),
    )
    out_specs = P("tile", None, "subap", None)
    return jax.shard_map(
        on_device, mesh=mesh, in_specs=in_specs, out_specs=out_specs, check_vma=False
    )
```

```python
import functools

import jax
import jax.numpy as jnp
from jax import lax
from jax.experimental import pallas as pl
from jax.experimental.pallas import tpu as pltpu
from jax.sharding import PartitionSpec as P

MESH = pl.DeviceIdType.MESH
LANES = 128
FLAG_ROWS = 16


def plan_kernel(dims, last, feet, offs, info):
    n, tdev, cap = dims
    for owner in range(n):
        first, second = feet[owner * cap], feet[owner * cap + 1]
        for slot in range(cap):
            entry = owner * cap + slot
            tile = jnp.maximum(first, second) if slot else jnp.minimum(first, second)
            start = offs[tile]
            base = jnp.minimum(lax.div(start, LANES), last)
            info[entry] = base
            info[n * cap + entry] = start - base * LANES
            info[2 * n * cap + entry] = tile - owner * tdev


def kernel(dims, info, pulses, azimuth, interp, out, block, az, table, send, recv, acc,
           zsend, zrecv, psend, precv, load_sem, column_sem, send_sem, recv_sem, zsend_sem, zrecv_sem, psend_sem, precv_sem):
    n, ns, tdev, cap = dims
    columns, rows = block.shape[:2]
    half = rows // 2
    width = recv.shape[2]
    ta, two_tr = acc.shape[1:]
    tr = two_tr // 2
    height = ta // ns
    me = lax.axis_index("tile")
    mz = lax.axis_index("subap")

    loads = [
        pltpu.make_async_copy(src, dst, load_sem.at[i])
        for i, (src, dst) in enumerate(((interp, table), (azimuth, az)))
    ]

    def column_copy(c):
        return pltpu.make_async_copy(
            pulses.at[:, pl.ds(pl.multiple_of(c * LANES, LANES), LANES)], block.at[c], column_sem.at[c]
        )

    def fetch(c, carry):
        column_copy(c).start()
        return carry

    def fetched(c, carry):
        column_copy(c).wait()
        return carry

    lax.fori_loop(0, columns, fetch, 0)
    for load in loads:
        load.start()

    barrier = pltpu.get_barrier_semaphore()
    for d in range(1, n):
        pl.semaphore_signal(barrier, inc=1, device_id={"tile": lax.rem(me + d, n)}, device_id_type=MESH)
    for e in range(1, ns):
        pl.semaphore_signal(barrier, inc=1, device_id={"subap": lax.rem(mz + e, ns)}, device_id_type=MESH)

    def at(slot):
        start = slot * rows + (FLAG_ROWS if slot > 0 else 0)
        size = rows + (FLAG_ROWS if slot == 0 else 0)
        return start, size

    def window_copy(d, slot):
        start, size = at(slot)
        return pltpu.make_async_remote_copy(
            src_ref=send.at[d, pl.ds(start, size)],
            dst_ref=recv.at[d, pl.ds(start, size)],
            send_sem=send_sem.at[d, slot],
            recv_sem=recv_sem.at[d, slot],
            device_id={"tile": lax.rem(me + d, n)},
            device_id_type=MESH,
        )

    taken = lax.broadcasted_iota(jnp.int32, (2 * LANES, LANES), 0) - lax.broadcasted_iota(
        jnp.int32, (2 * LANES, LANES), 1
    )
    flag_row = lax.broadcasted_iota(jnp.int32, (FLAG_ROWS, width), 0)

    def cut(d, slot):
        owner = lax.rem(me + d, n)
        entry = owner * cap + slot
        base, shift = info[entry], info[n * cap + entry]
        pick = jnp.where(taken == shift, 1.0, 0.0).astype(jnp.bfloat16)
        place = at(slot)[0]
        x = [block[base + c] for c in range(width // LANES + 1)]
        for c in range(width // LANES):
            pair = jnp.concatenate(x[c:c + 2], axis=1)
            y = jnp.dot(pair, pick, preferred_element_type=jnp.float32)
            send[d, pl.ds(place, rows), c * LANES:(c + 1) * LANES] = y.astype(jnp.bfloat16)
        if slot == 0:
            low, high = info[2 * n * cap + entry], info[2 * n * cap + entry + 1]
            hit = (flag_row == low) | (flag_row == tdev + high)
            send[d, pl.ds(rows, FLAG_ROWS)] = jnp.where(hit, 1.0, 0.0).astype(jnp.bfloat16)

    lax.fori_loop(0, columns, fetched, 0)
    pl.semaphore_wait(barrier, n + ns - 2)
    for slot in range(cap):
        def issue(i, carry, slot=slot):
            cut(n - i, slot)
            if slot == 0:
                window_copy(n - i, slot).start()
            return carry
        lax.fori_loop(1, n, issue, 0)
    for slot in range(cap):
        cut(0, slot)
    for load in loads:
        load.wait()

    def add(buf, d, t):
        flags = buf[d, pl.ds(rows, FLAG_ROWS)].astype(jnp.float32)
        w = None
        for slot in range(cap):
            if slot <= t <= tdev - cap + slot:
                row = slot * tdev + t
                term = buf[d, pl.ds(at(slot)[0], rows)] * flags[row:row + 1].astype(jnp.bfloat16)
                w = term if w is None else w + term
        pr = jnp.dot(w, table[t, 0], preferred_element_type=jnp.float32)
        pi = jnp.dot(w, table[t, 1], preferred_element_type=jnp.float32)
        rr = (pr[:half] - pi[half:]).astype(jnp.bfloat16)
        ri = (pi[:half] + pr[half:]).astype(jnp.bfloat16)
        right = jnp.concatenate(
            [jnp.concatenate([rr, ri], axis=1), jnp.concatenate([-ri, rr], axis=1)], axis=0
        )
        k = lax.rem(me - d + n, n)
        left = jnp.concatenate([az[t, k, 0], az[t, k, 1]], axis=1)
        return jnp.dot(left, right, preferred_element_type=jnp.float32)

    def image_copy(e, t):
        dest = lax.rem(mz + e, ns)
        return pltpu.make_async_remote_copy(
            src_ref=zsend.at[t, pl.ds(pl.multiple_of(dest * height, height), height)],
            dst_ref=zrecv.at[e, t],
            send_sem=zsend_sem.at[e, t],
            recv_sem=zrecv_sem.at[e, t],
            device_id={"subap": dest},
            device_id_type=MESH,
        )

    for t in range(tdev):
        acc[t] = add(send, 0, t)
    for slot in range(cap):
        if slot + 1 < cap:
            def follow(i, carry, slot=slot):
                window_copy(n - i, slot).wait_send()
                window_copy(n - i, slot + 1).start()
                return carry
            lax.fori_loop(1, n, follow, 0)
        done = [t for t in range(tdev) if min(t, cap - 1) == slot]

        for t in done:
            def gather(d, carry, slot=slot, t=t, first=t == done[0]):
                if first:
                    window_copy(d, slot).wait_recv()
                acc[t] += add(recv, d, t)
                return carry
            lax.fori_loop(1, n, gather, 0)
            zsend[t] = acc[t].astype(jnp.bfloat16)
            for e in range(1, ns):
                image_copy(e, t).start()

    own = pl.ds(pl.multiple_of(mz * height, height), height)
    raw = []
    for t in range(tdev):
        x = acc[t, own]
        for e in range(1, ns):
            image_copy(e, t).wait_recv()
            x = x + zrecv[e, t].astype(jnp.float32)
        zraw = jnp.sum(x * x, axis=0, keepdims=True)
        fold = sum(zraw[:, c:c + LANES] for c in range(0, two_tr, LANES))
        psend[t] = jnp.broadcast_to(fold, (8, LANES))
        acc[t, own] = x

    def power_copy(e):
        return pltpu.make_async_remote_copy(
            src_ref=psend,
            dst_ref=precv.at[e],
            send_sem=psend_sem.at[e],
            recv_sem=precv_sem.at[e],
            device_id={"subap": lax.rem(mz + e, ns)},
            device_id_type=MESH,
        )

    for e in range(1, ns):
        power_copy(e).start()
    for e in range(1, ns):
        power_copy(e).wait_recv()
    for t in range(tdev):
        total = psend[t]
        for e in range(1, ns):
            total = total + precv[e, t]
        power = jnp.sum(total[:1], axis=1, keepdims=True) / (ta * two_tr)
        x = acc[t, own] / jnp.sqrt(power + 1e-06)
        out[t, 0] = x[:, :tr]
        out[t, 1] = x[:, tr:]

    def drain(d, carry):
        window_copy(d, cap - 1).wait_send()
        return carry
    lax.fori_loop(1, n, drain, 0)
    for e in range(1, ns):
        power_copy(e).wait_send()
        for t in range(tdev):
            image_copy(e, t).wait_send()


def on_device(pulses, footprint, offsets, azimuth, range_interp):
    n, ns = lax.axis_size("tile"), lax.axis_size("subap")
    tdev = azimuth.shape[0]
    cap = footprint.shape[2] // n
    rows = 2 * pulses.shape[3]
    width, tr = range_interp.shape[2:]
    ta = azimuth.shape[4]
    height = ta // ns
    stage = cap * rows + FLAG_ROWS
    columns = pulses.shape[4] // LANES
    dma = pltpu.SemaphoreType.DMA
    smem = pl.BlockSpec(memory_space=pltpu.SMEM)
    hbm = pl.BlockSpec(memory_space=pl.ANY)
    info = pl.pallas_call(
        functools.partial(plan_kernel, (n, tdev, cap), columns - width // LANES - 1),
        out_shape=jax.ShapeDtypeStruct((3 * n * cap,), jnp.int32),
        in_specs=[smem, smem],
        out_specs=smem,
    )(footprint.reshape(-1), offsets)
    return pl.pallas_call(
        functools.partial(kernel, (n, ns, tdev, cap)),
        out_shape=jax.ShapeDtypeStruct((tdev, 2, height, tr), jnp.float32),
        in_specs=[smem, hbm, hbm, hbm],
        out_specs=pl.BlockSpec(memory_space=pltpu.VMEM),
        scratch_shapes=[
            pltpu.VMEM((columns, rows, LANES), jnp.bfloat16),
            pltpu.VMEM((tdev, n, 2, ta, rows // 2), jnp.bfloat16),
            pltpu.VMEM((tdev, 2, width, tr), jnp.bfloat16),
            pltpu.VMEM((n, stage, width), jnp.bfloat16),
            pltpu.VMEM((n, stage, width), jnp.bfloat16),
            pltpu.VMEM((tdev, ta, 2 * tr), jnp.float32),
            pltpu.VMEM((tdev, ta, 2 * tr), jnp.bfloat16),
            pltpu.VMEM((ns, tdev, height, 2 * tr), jnp.bfloat16),
            pltpu.VMEM((tdev, 8, LANES), jnp.float32),
            pltpu.VMEM((ns, tdev, 8, LANES), jnp.float32),
            dma((2,)),
            dma((columns,)),
            dma((n, cap)),
            dma((n, cap)),
            dma((ns, tdev)),
            dma((ns, tdev)),
            dma((ns,)),
            dma((ns,)),
        ],
        compiler_params=pltpu.CompilerParams(
            collective_id=0, has_side_effects=True, vmem_limit_bytes=62 * 1024 * 1024
        ),
        cost_estimate=pl.CostEstimate(flops=5_000_000_000, bytes_accessed=14_000_000, transcendentals=0),
    )(info, pulses.reshape(rows, pulses.shape[4]), azimuth[:, :, 0], range_interp)


def solution(mesh):
    in_specs = (
        P("tile", "subap", None, None, None),
        P("tile", "subap", None),
        P(),
        P("tile", None, "subap", None, None, None),
        P("tile", None, None, None),
    )
    out_specs = P("tile", None, "subap", None)
    return jax.shard_map(
        on_device, mesh=mesh, in_specs=in_specs, out_specs=out_specs, check_vma=False
    )
```

```python
import functools

import jax
import jax.numpy as jnp
from jax import lax
from jax.experimental import pallas as pl
from jax.experimental.pallas import tpu as pltpu
from jax.sharding import PartitionSpec as P

MESH = pl.DeviceIdType.MESH
LANES = 128
FLAG_ROWS = 16


def plan_kernel(dims, last, feet, offs, info):
    n, tdev, cap = dims
    for owner in range(n):
        first, second = feet[owner * cap], feet[owner * cap + 1]
        for slot in range(cap):
            entry = owner * cap + slot
            tile = jnp.maximum(first, second) if slot else jnp.minimum(first, second)
            start = offs[tile]
            base = jnp.minimum(lax.div(start, LANES), last)
            info[entry] = base
            info[n * cap + entry] = start - base * LANES
            info[2 * n * cap + entry] = tile - owner * tdev


def kernel(dims, info, pulses, azimuth, interp, out, block, az, table, send, recv, acc,
           zsend, zrecv, psend, precv, load_sem, column_sem, send_sem, recv_sem, zsend_sem, zrecv_sem, psend_sem, precv_sem):
    n, ns, tdev, cap = dims
    columns, rows = block.shape[:2]
    half = rows // 2
    width = recv.shape[2]
    ta, two_tr = acc.shape[1:]
    tr = two_tr // 2
    height = ta // ns
    me = lax.axis_index("tile")
    mz = lax.axis_index("subap")

    loads = [
        pltpu.make_async_copy(src, dst, load_sem.at[i])
        for i, (src, dst) in enumerate(((interp, table), (azimuth, az)))
    ]

    def column_copy(c):
        return pltpu.make_async_copy(
            pulses.at[:, pl.ds(pl.multiple_of(c * LANES, LANES), LANES)], block.at[c], column_sem.at[c]
        )

    def fetch(c, carry):
        column_copy(c).start()
        return carry

    def fetched(c, carry):
        column_copy(c).wait()
        return carry

    lax.fori_loop(0, columns, fetch, 0)
    for load in loads:
        load.start()

    barrier = pltpu.get_barrier_semaphore()
    for d in range(1, n):
        pl.semaphore_signal(barrier, inc=1, device_id={"tile": lax.rem(me + d, n)}, device_id_type=MESH)
    for e in range(1, ns):
        pl.semaphore_signal(barrier, inc=1, device_id={"subap": lax.rem(mz + e, ns)}, device_id_type=MESH)

    def at(slot):
        start = slot * rows + (FLAG_ROWS if slot > 0 else 0)
        size = rows + (FLAG_ROWS if slot == 0 else 0)
        return start, size

    def window_copy(d, slot):
        start, size = at(slot)
        return pltpu.make_async_remote_copy(
            src_ref=send.at[d, pl.ds(start, size)],
            dst_ref=recv.at[d, pl.ds(start, size)],
            send_sem=send_sem.at[d, slot],
            recv_sem=recv_sem.at[d, slot],
            device_id={"tile": lax.rem(me + d, n)},
            device_id_type=MESH,
        )

    taken = lax.broadcasted_iota(jnp.int32, (2 * LANES, LANES), 0) - lax.broadcasted_iota(
        jnp.int32, (2 * LANES, LANES), 1
    )
    flag_row = lax.broadcasted_iota(jnp.int32, (FLAG_ROWS, width), 0)

    def cut(d, slot):
        owner = lax.rem(me + d, n)
        entry = owner * cap + slot
        base, shift = info[entry], info[n * cap + entry]
        pick = jnp.where(taken == shift, 1.0, 0.0).astype(jnp.bfloat16)
        place = at(slot)[0]
        x = [block[base + c] for c in range(width // LANES + 1)]
        for c in range(width // LANES):
            pair = jnp.concatenate(x[c:c + 2], axis=1)
            y = jnp.dot(pair, pick, preferred_element_type=jnp.float32)
            send[d, pl.ds(place, rows), c * LANES:(c + 1) * LANES] = y.astype(jnp.bfloat16)
        if slot == 0:
            low, high = info[2 * n * cap + entry], info[2 * n * cap + entry + 1]
            hit = (flag_row == low) | (flag_row == tdev + high)
            send[d, pl.ds(rows, FLAG_ROWS)] = jnp.where(hit, 1.0, 0.0).astype(jnp.bfloat16)

    lax.fori_loop(0, columns, fetched, 0)
    pl.semaphore_wait(barrier, n + ns - 2)
    for slot in range(cap):
        def issue(i, carry, slot=slot):
            cut(n - i, slot)
            if slot == 0:
                window_copy(n - i, slot).start()
            return carry
        lax.fori_loop(1, n, issue, 0)
    for slot in range(cap):
        cut(0, slot)
    for load in loads:
        load.wait()

    def add(buf, d, t):
        flags = buf[d, pl.ds(rows, FLAG_ROWS)].astype(jnp.float32)
        w = None
        for slot in range(cap):
            if slot <= t <= tdev - cap + slot:
                row = slot * tdev + t
                term = buf[d, pl.ds(at(slot)[0], rows)] * flags[row:row + 1].astype(jnp.bfloat16)
                w = term if w is None else w + term
        pr = jnp.dot(w, table[t, 0], preferred_element_type=jnp.float32)
        pi = jnp.dot(w, table[t, 1], preferred_element_type=jnp.float32)
        rr = (pr[:half] - pi[half:]).astype(jnp.bfloat16)
        ri = (pi[:half] + pr[half:]).astype(jnp.bfloat16)
        right = jnp.concatenate(
            [jnp.concatenate([rr, ri], axis=1), jnp.concatenate([-ri, rr], axis=1)], axis=0
        )
        k = lax.rem(me - d + n, n)
        left = jnp.concatenate([az[t, k, 0], az[t, k, 1]], axis=1)
        return jnp.dot(left, right, preferred_element_type=jnp.float32)

    def image_copy(e, t):
        dest = lax.rem(mz + e, ns)
        return pltpu.make_async_remote_copy(
            src_ref=zsend.at[t, pl.ds(pl.multiple_of(dest * height, height), height)],
            dst_ref=zrecv.at[e, t],
            send_sem=zsend_sem.at[e, t],
            recv_sem=zrecv_sem.at[e, t],
            device_id={"subap": dest},
            device_id_type=MESH,
        )

    for t in range(tdev):
        acc[t] = add(send, 0, t)
    for slot in range(cap):
        if slot + 1 < cap:
            def follow(i, carry, slot=slot):
                window_copy(n - i, slot).wait_send()
                window_copy(n - i, slot + 1).start()
                return carry
            lax.fori_loop(1, n, follow, 0)
        done = [t for t in range(tdev) if min(t, cap - 1) == slot]

        for t in done:
            def gather(i, carry, slot=slot, t=t, first=t == done[0]):
                d = n - i
                if first:
                    window_copy(d, slot).wait_recv()
                acc[t] += add(recv, d, t)
                return carry
            lax.fori_loop(1, n, gather, 0)
            zsend[t] = acc[t].astype(jnp.bfloat16)
            for e in range(1, ns):
                image_copy(e, t).start()

    own = pl.ds(pl.multiple_of(mz * height, height), height)
    raw = []
    for t in range(tdev):
        x = acc[t, own]
        for e in range(1, ns):
            image_copy(e, t).wait_recv()
            x = x + zrecv[e, t].astype(jnp.float32)
        zraw = jnp.sum(x * x, axis=0, keepdims=True)
        fold = sum(zraw[:, c:c + LANES] for c in range(0, two_tr, LANES))
        psend[t] = jnp.broadcast_to(fold, (8, LANES))
        acc[t, own] = x

    def power_copy(e):
        return pltpu.make_async_remote_copy(
            src_ref=psend,
            dst_ref=precv.at[e],
            send_sem=psend_sem.at[e],
            recv_sem=precv_sem.at[e],
            device_id={"subap": lax.rem(mz + e, ns)},
            device_id_type=MESH,
        )

    for e in range(1, ns):
        power_copy(e).start()
    for e in range(1, ns):
        power_copy(e).wait_recv()
    for t in range(tdev):
        total = psend[t]
        for e in range(1, ns):
            total = total + precv[e, t]
        power = jnp.sum(total[:1], axis=1, keepdims=True) / (ta * two_tr)
        x = acc[t, own] / jnp.sqrt(power + 1e-06)
        out[t, 0] = x[:, :tr]
        out[t, 1] = x[:, tr:]

    def drain(d, carry):
        window_copy(d, cap - 1).wait_send()
        return carry
    lax.fori_loop(1, n, drain, 0)
    for e in range(1, ns):
        power_copy(e).wait_send()
        for t in range(tdev):
            image_copy(e, t).wait_send()


def on_device(pulses, footprint, offsets, azimuth, range_interp):
    n, ns = lax.axis_size("tile"), lax.axis_size("subap")
    tdev = azimuth.shape[0]
    cap = footprint.shape[2] // n
    rows = 2 * pulses.shape[3]
    width, tr = range_interp.shape[2:]
    ta = azimuth.shape[4]
    height = ta // ns
    stage = cap * rows + FLAG_ROWS
    columns = pulses.shape[4] // LANES
    dma = pltpu.SemaphoreType.DMA
    smem = pl.BlockSpec(memory_space=pltpu.SMEM)
    hbm = pl.BlockSpec(memory_space=pl.ANY)
    info = pl.pallas_call(
        functools.partial(plan_kernel, (n, tdev, cap), columns - width // LANES - 1),
        out_shape=jax.ShapeDtypeStruct((3 * n * cap,), jnp.int32),
        in_specs=[smem, smem],
        out_specs=smem,
    )(footprint.reshape(-1), offsets)
    return pl.pallas_call(
        functools.partial(kernel, (n, ns, tdev, cap)),
        out_shape=jax.ShapeDtypeStruct((tdev, 2, height, tr), jnp.float32),
        in_specs=[smem, hbm, hbm, hbm],
        out_specs=pl.BlockSpec(memory_space=pltpu.VMEM),
        scratch_shapes=[
            pltpu.VMEM((columns, rows, LANES), jnp.bfloat16),
            pltpu.VMEM((tdev, n, 2, ta, rows // 2), jnp.bfloat16),
            pltpu.VMEM((tdev, 2, width, tr), jnp.bfloat16),
            pltpu.VMEM((n, stage, width), jnp.bfloat16),
            pltpu.VMEM((n, stage, width), jnp.bfloat16),
            pltpu.VMEM((tdev, ta, 2 * tr), jnp.float32),
            pltpu.VMEM((tdev, ta, 2 * tr), jnp.bfloat16),
            pltpu.VMEM((ns, tdev, height, 2 * tr), jnp.bfloat16),
            pltpu.VMEM((tdev, 8, LANES), jnp.float32),
            pltpu.VMEM((ns, tdev, 8, LANES), jnp.float32),
            dma((2,)),
            dma((columns,)),
            dma((n, cap)),
            dma((n, cap)),
            dma((ns, tdev)),
            dma((ns, tdev)),
            dma((ns,)),
            dma((ns,)),
        ],
        compiler_params=pltpu.CompilerParams(
            collective_id=0, has_side_effects=True, vmem_limit_bytes=62 * 1024 * 1024
        ),
        cost_estimate=pl.CostEstimate(flops=5_000_000_000, bytes_accessed=14_000_000, transcendentals=0),
    )(info, pulses.reshape(rows, pulses.shape[4]), azimuth[:, :, 0], range_interp)


def solution(mesh):
    in_specs = (
        P("tile", "subap", None, None, None),
        P("tile", "subap", None),
        P(),
        P("tile", None, "subap", None, None, None),
        P("tile", None, None, None),
    )
    out_specs = P("tile", None, "subap", None)
    return jax.shard_map(
        on_device, mesh=mesh, in_specs=in_specs, out_specs=out_specs, check_vma=False
    )
```
